256 devices in a mesh: seq: 32 (over x, z_hi, core), mp: 8 (over z_lo, y).
Axes of the slice: x: 4, y: 4, z: 8 (z_hi: 4, z_lo: 2; z = z_hi * 2 + z_lo), core: 2. Of those that a mesh axis runs over, the one named last changes fastest.
Arguments:
- activations: bfloat16 [131072, 4096], P('seq', 'mp'), may hold values from -6 to 6
- conv_weight: float32 [3, 4096], P(None, 'mp'), may hold values from -3.5 to 3.5
- chan_right: bfloat16 [64, 64, 64], P('mp'), may hold values from -0.75 to 0.75
- chan_left: bfloat16 [64, 64, 64], P('mp'), may hold values from -0.75 to 0.75
- row_factor: bfloat16 [512, 512], replicated, may hold values from -0.25 to 0.25
- col_factor: bfloat16 [256, 256], replicated, may hold values from -0.375 to 0.375
- twiddle_one: float32 [256, 512], P('seq'), may hold values from -2 to 2
- twiddle_two: float32 [256, 512], P(None, 'seq'), may hold values from -2 to 2
- spectrum: bfloat16 [256, 512, 4096], P(None, 'seq', 'mp'), may hold values from -6 to 6
Outputs:
- result: bfloat16 [131072, 4096], P('seq', 'mp')
The draws below stay inside these ranges and needn't reach their ends.
All inputs are finite; a program needn't handle non-finite values.
Results may differ from the reference program's by a relative error of at most 0.0085.
Values may be sent and summed in bfloat16 or wider, within the bound.
A program may use at most 128 MiB of HBM per device.

```python
import jax
import jax.numpy as jnp
from jax import lax

A = 256
B = 512
CB = 64
D = 4096


def block_scale(rng, dims, pieces, least, largest):
    def one(dim, shards_of):
        steps = jax.random.uniform(jax.random.fold_in(jax.random.fold_in(rng, 6), dim), (shards_of,), jnp.float32, least / len(pieces), largest / len(pieces))
        return jnp.repeat(jnp.exp(steps), dims[dim] // shards_of).reshape((-1,) + (1,) * (len(dims) - dim - 1))

    level = one(*pieces[0])
    for cut in pieces[1:]:
        level = level * one(*cut)
    return level


def noise(own_key, dims, deviation, limit, cuts=(), kind=jnp.bfloat16):
    loudness = block_scale(own_key, dims, cuts, -0.22, 0.18) if cuts else 1.0
    values = jax.random.normal(own_key, dims, jnp.float32) * deviation * loudness
    return jnp.minimum(jnp.maximum(values, -limit), limit).astype(kind)


def setup_inputs(seed: int = 0) -> dict:
    key_of = jax.random.split(jax.random.key(seed), 10)
    return {
        "activations": noise(key_of[0], (A * B, D), 1.0, 6.0, ((0, 32), (1, 8))),
        "conv_weight": noise(key_of[1], (3, D), 3 ** -0.5, 3.5, ((1, 8),), jnp.float32),
        "chan_right": noise(key_of[2], (CB, CB, CB), CB ** -0.5, 0.75, ((0, 8),)),
        "chan_left": noise(key_of[3], (CB, CB, CB), CB ** -0.5, 0.75, ((0, 8),)),
        "row_factor": noise(key_of[4], (B, B), B ** -0.5, 0.25),
        "col_factor": noise(key_of[5], (A, A), A ** -0.5, 0.375),
        "twiddle_one": jnp.clip(jax.random.uniform(key_of[6], (A, B), jnp.float32, -2.0, 2.0) * block_scale(key_of[6], (A, B), ((0, 32),), -0.4, 0.0), -2.0, 2.0),
        "twiddle_two": jnp.clip(jax.random.uniform(key_of[7], (A, B), jnp.float32, -2.0, 2.0) * block_scale(key_of[7], (A, B), ((1, 32),), -0.4, 0.0), -2.0, 2.0),
        "spectrum": noise(key_of[8], (A, B, D), 1.0, 6.0, ((1, 32), (2, 8))),
    }


def round_half(value):
    return lax.optimization_barrier(value.astype(jnp.bfloat16)).astype(jnp.float32)


def front(window, conv_weight, chan_right, chan_left):
    x_float = window.astype(jnp.float32)
    taps = conv_weight.astype(jnp.float32)
    conv_out = taps[0] * x_float[2:] + taps[1] * x_float[1:-1] + taps[2] * x_float[:-2]
    gated = round_half(x_float[2:] * jax.nn.silu(conv_out))
    gated = gated.reshape(gated.shape[0], CB, CB)
    first = round_half(jnp.einsum("nij,ijk->nik", gated, chan_right.astype(jnp.float32)))
    second = jnp.einsum("nik,kil->nlk", first, chan_left.astype(jnp.float32))
    return second.astype(jnp.bfloat16).reshape(second.shape[0], D)


def reference(activations, conv_weight, chan_right, chan_left, row_factor, col_factor, twiddle_one, twiddle_two, spectrum):
    total = A * B
    token_block = min(total, 4096)
    padded = jnp.concatenate([jnp.zeros((2, D), jnp.bfloat16), activations], axis=0)
    starts = jnp.arange(total // token_block, dtype=jnp.int32) * token_block
    zero_index = jnp.zeros((), jnp.int32)

    def one_block(start):
        window = lax.dynamic_slice(padded, (start.astype(jnp.int32), zero_index), (token_block + 2, D))
        return front(window, conv_weight, chan_right, chan_left)

    mixed_in = lax.map(one_block, starts).reshape(A, B, D)
    chan_block = min(D, 512)
    count = D // chan_block

    def split(array):
        return jnp.moveaxis(array.reshape(A, B, count, chan_block), 2, 0)

    row_float = row_factor.astype(jnp.float32)
    col_float = col_factor.astype(jnp.float32)

    def mixing(parts):
        grid, kernel, initial = parts
        rows_out = round_half(jnp.einsum("pb,abc->apc", row_float, grid.astype(jnp.float32)) * twiddle_one[:, :, None])
        spectral = round_half(jnp.einsum("qa,apc->qpc", col_float, rows_out) * kernel.astype(jnp.float32))
        back = round_half(jnp.einsum("qa,qpc->apc", col_float, spectral) * twiddle_two[:, :, None])
        mixed = jnp.einsum("pb,apc->abc", row_float, back)
        return (initial.astype(jnp.float32) + mixed).astype(jnp.bfloat16)

    blocks = lax.map(mixing, (split(mixed_in), split(spectrum), split(activations)))
    return jnp.moveaxis(blocks, 0, 2).reshape(total, D)
```

```python
import jax
import jax.numpy as jnp
from jax import lax
from jax.experimental import pallas as pl
from jax.experimental.pallas import tpu as pltpu
from jax.sharding import PartitionSpec as P

MESH = pl.DeviceIdType.MESH


def shifted(block, axis, distance):
    devices = range(lax.axis_size(axis))
    route = [(i - distance, i) for i in devices if i - distance in devices]
    return lax.ppermute(block, axis, route)


def dot32(a, b):
    return jnp.dot(a, b, preferred_element_type=jnp.float32)


def iota(shape, dim):
    return lax.broadcasted_iota(jnp.int32, shape, dim)


def right_matrix(chan_right):
    groups, width, _ = chan_right.shape
    size = groups * width
    col = iota((width, size), 1)
    spread = (iota((width, size), 0) == col // 128 * 16 + col % 16).astype(jnp.bfloat16)
    full = dot32(chan_right.reshape(size, width), spread)
    same = iota((size, size), 0) // width == iota((size, size), 1) % 128 // 16
    return jnp.where(same, full, 0.0).astype(jnp.bfloat16)


def left_matrices(chan_left):
    width = chan_left.shape[0]
    size = width * 16
    packed = chan_left.reshape(width // 16, 16, width, width).transpose(0, 2, 1, 3)
    spread = (iota((width, size), 0) == iota((width, size), 1) // 16).astype(jnp.bfloat16)
    full = dot32(packed.reshape(width // 16 * size, width), spread)
    full = full.reshape(width // 16, size, size)
    same = iota((size, size), 0) % 16 == iota((size, size), 1) % 16
    return jnp.where(same, full, 0.0).astype(jnp.bfloat16)


def natural_order():
    row, col = iota((512, 512), 0), iota((512, 512), 1)
    target = row // 16 % 8 * 64 + row // 128 * 16 + row % 16
    return (target == col).astype(jnp.bfloat16)


def exchange_kernel(x_ref, out_ref, local_sem, send_sem, recv_sem):
    seq, mp = lax.axis_index("seq"), lax.axis_index("mp")
    me = seq * 8 + mp

    def partner(step):
        z = (seq // 2 % 4) * 2 + mp // 4
        z = (z + step) % 8
        rest = step // 8
        core = (seq + rest) % 2
        x = (seq // 8 + rest // 2) % 4
        y = (mp + rest // 8) % 4
        return (x * 4 + z // 2) * 2 + core, z % 2 * 4 + y

    barrier = pltpu.get_barrier_semaphore()

    @pl.loop(1, 256)
    def _(step):
        pl.semaphore_signal(barrier, inc=1, device_id=partner(step), device_id_type=MESH)

    own = pltpu.make_async_copy(x_ref.at[me], out_ref.at[me], local_sem)
    own.start()
    pl.semaphore_wait(barrier, 255)

    @pl.loop(1, 256)
    def _(step):
        to_seq, to_mp = partner(step)
        pltpu.make_async_remote_copy(
            src_ref=x_ref.at[to_seq * 8 + to_mp],
            dst_ref=out_ref.at[me],
            send_sem=send_sem,
            recv_sem=recv_sem,
            device_id=(to_seq, to_mp),
            device_id_type=MESH,
        ).start()

    own.wait()
    others = out_ref.at[pl.ds(0, 255)]
    pltpu.make_async_copy(others, others, recv_sem).wait()
    pltpu.make_async_copy(others, others, send_sem).wait()


def exchange(x):
    return pl.pallas_call(
        exchange_kernel,
        name="exchange",
        out_shape=jax.ShapeDtypeStruct(x.shape, x.dtype),
        in_specs=[pl.BlockSpec(memory_space=pltpu.VMEM)],
        out_specs=pl.BlockSpec(memory_space=pltpu.VMEM),
        scratch_shapes=[pltpu.SemaphoreType.DMA] * 3,
        compiler_params=pltpu.CompilerParams(
            collective_id=0, has_side_effects=True, vmem_limit_bytes=16 << 20
        ),
    )(x)


def shards(
    activations,
    conv_weight,
    chan_right,
    chan_left,
    row_factor,
    col_factor,
    twiddle_one,
    twiddle_two,
    spectrum,
):
    token_count, local_width = activations.shape
    row_count, block_len = twiddle_one.shape
    x_float = activations.astype(jnp.float32)
    carried = shifted(activations[token_count - 2 :], "seq", 1)
    extended = jnp.concatenate([carried.astype(jnp.float32), x_float], axis=0)
    conv_out = (
        conv_weight[0] * extended[2:]
        + conv_weight[1] * extended[1:-1]
        + conv_weight[2] * extended[:-2]
    )
    gated = (x_float * jax.nn.silu(conv_out)).astype(jnp.bfloat16)
    chan_left = lax.all_gather(chan_left, "mp", tiled=True)
    lefts = left_matrices(chan_left)
    first = dot32(gated, right_matrix(chan_right)).astype(jnp.bfloat16)
    first = first.reshape(row_count, block_len, local_width)
    rows_out = jnp.einsum("pb,abc->apc", row_factor, first, preferred_element_type=jnp.float32)
    rows_out = (rows_out * twiddle_one[:, :, None]).astype(jnp.bfloat16)
    turned = lax.all_to_all(rows_out, "mp", split_axis=0, concat_axis=0, tiled=True)
    parts = []
    for k in range(4):
        block = turned[:, :, k * 128 : (k + 1) * 128].transpose(1, 0, 2).reshape(block_len, 1024)
        parts.append(dot32(block, lefts[k]).astype(jnp.bfloat16).reshape(block_len, 8, 128))
    mixed = jnp.concatenate(parts, axis=2)
    mixed = jnp.einsum("pmc,cd->pmd", mixed, natural_order(), preferred_element_type=jnp.float32)
    mixed = mixed.astype(jnp.bfloat16).reshape(32, 16, 8, 512).transpose(0, 2, 1, 3)
    columns = exchange(mixed.reshape(256, 16, 512))
    spectral = jnp.einsum("qa,apc->qpc", col_factor, columns, preferred_element_type=jnp.float32)
    spectral = (spectral * spectrum).astype(jnp.bfloat16)
    back = jnp.einsum("qa,qpc->apc", col_factor, spectral, preferred_element_type=jnp.float32)
    back = (back * twiddle_two[:, :, None]).astype(jnp.bfloat16)
    back = lax.all_to_all(
        back.reshape(32, 8, 16, 512), "seq", split_axis=0, concat_axis=0, tiled=True
    )
    mixed = jnp.einsum(
        "pb,apc->abc",
        row_factor,
        back.transpose(1, 0, 2, 3).reshape(row_count, block_len, local_width),
        preferred_element_type=jnp.float32,
    )
    result = x_float.reshape(row_count, block_len, local_width) + mixed
    return result.astype(jnp.bfloat16).reshape(token_count, local_width)


def solution(mesh):
    in_specs = (
        P("seq", "mp"),
        P(None, "mp"),
        P("mp", None, None),
        P("mp", None, None),
        P(),
        P(),
        P("seq", None),
        P(None, "seq"),
        P(None, "seq", "mp"),
    )
    out_specs = P("seq", "mp")
    return jax.shard_map(shards, mesh=mesh, in_specs=in_specs, out_specs=out_specs, check_vma=False)
```

```python
import jax
import jax.numpy as jnp
from jax import lax
from jax.experimental import pallas as pl
from jax.experimental.pallas import tpu as pltpu
from jax.sharding import PartitionSpec as P

MESH = pl.DeviceIdType.MESH
BF16 = jnp.bfloat16
F32 = jnp.float32


def dot32(a, b):
    return jnp.dot(a, b, preferred_element_type=F32)


def iota(shape, dim):
    return lax.broadcasted_iota(jnp.int32, shape, dim)


def one_hot(condition):
    return jnp.where(condition, 1.0, 0.0).astype(BF16)


def wait_bytes(ref, sem):
    pltpu.make_async_copy(ref, ref, sem).wait()


def kernel(
    x_hbm,
    taps,
    right_hbm,
    left_hbm,
    row_hbm,
    col_hbm,
    twiddle_one,
    twiddle_two,
    spectrum_hbm,
    out_hbm,
    xw,
    right,
    left_own,
    left_all,
    row_f,
    row_t,
    col_f,
    col_t,
    swap,
    natural,
    right_w,
    left_w,
    twiddle_b,
    gated,
    send_a,
    recv_a,
    mixed,
    send_b,
    recv_b,
    columns,
    kernel_t,
    send_c,
    recv_c,
    load_sem,
    x_sem,
    tail_sem,
    halo_send,
    halo_recv,
    left_send,
    left_recv,
    a_send,
    a_recv,
    a_own,
    b_send,
    b_recv,
    b_own,
    c_send,
    c_recv,
    c_own,
    out_sem,
):
    seq, mp = lax.axis_index("seq"), lax.axis_index("mp")
    x, z_hi, core = seq // 8, seq // 2 % 4, seq % 2
    z_lo, y = mp // 4, mp % 4
    me = seq * 8 + mp

    def partner(step):
        z = (z_hi * 2 + z_lo + step) % 8
        rest = step // 8
        to_core = (core + rest) % 2
        to_x = (x + rest // 2) % 4
        to_y = (y + rest // 8) % 4
        return (to_x * 4 + z // 2) * 2 + to_core, z % 2 * 4 + to_y

    def mp_peer(turn):
        return (z_lo + 1 + turn // 4) % 2 * 4 + (y + turn + 1) % 4

    barrier = pltpu.get_barrier_semaphore()

    small = [
        pltpu.make_async_copy(src, dst, load_sem.at[i])
        for i, (src, dst) in enumerate(
            ((right_hbm, right), (row_hbm, row_f), (col_hbm, col_f), (left_hbm, left_own))
        )
    ]
    for copy in small:
        copy.start()

    def x_copy(a):
        return pltpu.make_async_copy(
            x_hbm.at[pl.ds(pl.multiple_of(a * 512, 512), 512)],
            xw.at[a, pl.ds(16, 512)],
            x_sem.at[a],
        )

    def tail_copy(a):
        return pltpu.make_async_copy(
            x_hbm.at[pl.ds(pl.multiple_of(a * 512 - 16, 16), 16)],
            xw.at[a, pl.ds(0, 16)],
            tail_sem.at[a],
        )

    @pl.loop(0, 8)
    def _(turn):
        a = mp_peer(turn)
        x_copy(a).start()

        @pl.when(a > 0)
        def _():
            tail_copy(a).start()

    kernel_copies = [
        pltpu.make_async_copy(
            spectrum_hbm.at[:, :, pl.ds(256 * ch, 256)], send_c.at[ch], load_sem.at[4 + ch]
        )
        for ch in range(2)
    ]
    for copy in kernel_copies:
        copy.start()

    @pl.loop(1, 256)
    def _(step):
        pl.semaphore_signal(barrier, inc=1, device_id=partner(step), device_id_type=MESH)

    small[0].wait()
    col = iota((64, 512), 1)
    full = dot32(right[...], one_hot(iota((64, 512), 0) == col // 128 * 16 + col % 128 // 8))
    same = iota((512, 512), 0) // 64 == iota((512, 512), 1) % 8
    right_w[...] = jnp.where(same, full, 0.0).astype(BF16)
    small[1].wait()
    small[2].wait()
    small[3].wait()

    pl.semaphore_wait(barrier, 255)
    halo = pltpu.make_async_remote_copy(
        src_ref=x_hbm.at[pl.ds(4080, 16)],
        dst_ref=xw.at[0, pl.ds(0, 16)],
        send_sem=halo_send,
        recv_sem=halo_recv,
        device_id=((seq + 1) % 32, mp),
        device_id_type=MESH,
    )
    halo.start()

    @pl.loop(0, 7)
    def _(turn):
        peer = mp_peer(turn)
        shift = jnp.where(turn < 4, jnp.where(z_lo == 1, 1, 3), 0)
        to_seq = (x * 4 + (z_hi + shift) % 4) * 2 + core
        pltpu.make_async_remote_copy(
            src_ref=left_own,
            dst_ref=left_all.at[mp],
            send_sem=left_send,
            recv_sem=left_recv,
            device_id=(to_seq, peer),
            device_id_type=MESH,
        ).start()

    def rows_at(part):
        return pl.multiple_of((x + part) % 4 * 128, 128)

    def send_rows(turn, part):
        a = mp_peer(turn)
        rows = pl.ds(rows_at(part), 128)
        pltpu.make_async_remote_copy(
            src_ref=send_a.at[a, rows],
            dst_ref=recv_a.at[mp, rows],
            send_sem=a_send,
            recv_sem=a_recv.at[part // 2],
            device_id=(seq, a),
            device_id_type=MESH,
        ).start()

    @pl.loop(0, 8)
    def _(turn):
        a = mp_peer(turn)
        x_copy(a).wait()

        @pl.when(a > 0)
        def _():
            tail_copy(a).wait()

        @pl.when(a == 0)
        def _():
            halo.wait_recv()

            @pl.when(seq == 0)
            def _():
                xw[0, pl.ds(0, 16)] = jnp.zeros((16, 512), BF16)

        @pl.loop(0, 4)
        def _(tile):
            start = pl.multiple_of(tile * 128, 128)
            window = xw[a, pl.ds(start, 144)].astype(F32)
            here = window[16:]
            conv_out = (
                taps[0:1] * here + taps[1:2] * window[15:143] + taps[2:3] * window[14:142]
            )
            gated[pl.ds(start, 128)] = (here * conv_out / (1.0 + jnp.exp(-conv_out))).astype(BF16)

        first = dot32(gated[...], right_w[...]).astype(BF16)
        scale = jnp.sum(jnp.where(iota((512, 8), 1) == a, twiddle_one[...], 0.0), 1, keepdims=True)
        send_a[a] = (dot32(row_f[...], first) * scale).astype(BF16)

        @pl.when(turn < 7)
        def _():
            send_rows(turn, 0)
            send_rows(turn, 1)

    own_rows = pltpu.make_async_copy(send_a.at[mp], recv_a.at[mp], a_own)
    own_rows.start()

    @pl.loop(0, 7)
    def _(turn):
        send_rows(turn, 2)
        send_rows(turn, 3)

    row_t[...] = row_f[...].astype(F32).T.astype(BF16)
    col_t[...] = col_f[...].astype(F32).T.astype(BF16)
    row, col = iota((256, 256), 0), iota((256, 256), 1)
    swap[...] = one_hot(row // 16 + row % 16 * 16 == col)
    row, col = iota((512, 512), 0), iota((512, 512), 1)
    natural[...] = one_hot(row // 16 % 8 * 64 + row // 128 * 16 + row % 16 == col)

    left_all[mp] = left_own[...]
    wait_bytes(left_all.at[pl.ds(0, 7)], left_recv)

    @pl.loop(0, 8)
    def _(owner):
        slab = left_all[owner].astype(F32).reshape(4, 8, 8, 128)
        slab = slab.swapaxes(0, 1).reshape(256, 128).astype(BF16)
        for u in range(2):
            spread = iota((128, 1024), 0) == iota((128, 1024), 1) // 16 + 64 * u
            full = dot32(slab, one_hot(spread))
            k = owner % 2 * 8 + 4 * u + iota((256, 1024), 0) // 8 % 4
            full = jnp.where(k == iota((256, 1024), 1) % 16, full, 0.0).astype(BF16)
            rows = pl.ds(pl.multiple_of((owner % 2 * 2 + u) * 32, 32), 32)
            left_w[owner // 2, :, rows] = full.reshape(8, 32, 1024)

    for ch in range(2):
        kernel_copies[ch].wait()

        @pl.loop(0, 16)
        def _(block):
            rows = pl.ds(pl.multiple_of(block * 16, 16), 16)
            turned = dot32(swap[...], send_c[ch, rows].reshape(256, 256)).astype(BF16)
            kernel_t[ch, :, rows] = turned.reshape(16, 16, 256)

    for p in range(16):
        twiddle_b[p] = jnp.broadcast_to(twiddle_two[:, p : p + 1], (256, 128))

    own_rows.wait()

    def send_columns(ch, half, to_mp):
        @pl.loop(0, 16)
        def _(i):
            part = 2 * half + i // 8
            to_z = (z_hi + i // 2) % 4
            to_core = (core + i) % 2
            to_seq = ((x + part) % 4 * 4 + to_z) * 2 + to_core
            rows = pl.ds(pl.multiple_of((to_z * 2 + to_core) * 16, 16), 16)
            src = send_b.at[ch, to_mp, part, rows]
            dst = recv_b.at[ch, me]
            own = jnp.logical_and(to_seq == seq, to_mp == mp)

            @pl.when(own)
            def _():
                pltpu.make_async_copy(src, dst, b_own.at[ch]).start()

            @pl.when(jnp.logical_not(own))
            def _():
                pltpu.make_async_remote_copy(
                    src_ref=src,
                    dst_ref=dst,
                    send_sem=b_send,
                    recv_sem=b_recv.at[ch],
                    device_id=(to_seq, to_mp),
                    device_id_type=MESH,
                ).start()

    for half in range(2):
        wait_bytes(recv_a.at[pl.ds(0, 7), pl.ds(0, 256)], a_recv.at[half])

        @pl.loop(0, 4)
        def _(group):
            lanes = pl.ds(pl.multiple_of(group * 128, 128), 128)
            block = jnp.concatenate(
                [
                    jnp.concatenate(
                        [recv_a[m, pl.ds(rows_at(2 * half + i), 128), lanes] for i in range(2)], 0
                    )
                    for m in range(8)
                ],
                1,
            )
            for n in range(4):
                cut = slice(256 * n, 256 * n + 256)
                weights = left_w[group, :, :, cut].reshape(1024, 256)
                mixed[group, :, cut] = dot32(block, weights).astype(BF16)

        @pl.loop(0, 8)
        def _(turn):
            to_mp = mp_peer(turn)
            lanes = pl.ds(pl.multiple_of(to_mp * 128, 128), 128)
            block = jnp.concatenate([mixed[group, :, lanes] for group in range(4)], 1)
            for ch in range(2):
                cut = slice(256 * ch, 256 * ch + 256)
                turned = dot32(block, natural[:, cut]).astype(BF16)
                send_b[ch, to_mp, pl.ds(2 * half, 2)] = turned.reshape(2, 128, 256)
            send_columns(0, half, to_mp)

        @pl.loop(0, 8)
        def _(turn):
            send_columns(1, half, mp_peer(turn))

    for ch in range(2):
        wait_bytes(recv_b.at[ch, pl.ds(0, 255)], b_recv.at[ch])
        wait_bytes(recv_b.at[ch, 0], b_own.at[ch])

        @pl.loop(0, 16)
        def _(block):
            rows = pl.ds(pl.multiple_of(block * 16, 16), 16)
            turned = dot32(swap[...], recv_b[ch, rows].reshape(256, 256)).astype(BF16)
            columns[:, rows] = turned.reshape(16, 16, 256)

        @pl.loop(0, 16)
        def _(p):
            spectral = (dot32(col_f[...], columns[p]) * kernel_t[ch, p].astype(F32)).astype(BF16)
            back = dot32(col_t[...], spectral)
            scale = twiddle_b[p]
            columns[p] = (back * jnp.concatenate([scale, scale], 1)).astype(BF16)

        @pl.loop(0, 16)
        def _(i):
            block = (seq // 2 + i) % 16
            rows = pl.ds(pl.multiple_of(block * 16, 16), 16)
            turned = dot32(swap[...], columns[:, rows].reshape(256, 256)).astype(BF16)
            send_c[ch, rows] = turned.reshape(16, 16, 256)
            for to_core in range(2):
                to_seq = block * 2 + to_core
                src = send_c.at[ch, pl.ds(pl.multiple_of(to_seq * 8, 8), 8)]
                dst = recv_c.at[ch, :, pl.ds(pl.multiple_of(seq * 16, 16), 16)]

                @pl.when(to_seq == seq)
                def _(src=src, dst=dst):
                    pltpu.make_async_copy(src, dst, c_own.at[ch]).start()

                @pl.when(to_seq != seq)
                def _(src=src, dst=dst, to_seq=to_seq):
                    pltpu.make_async_remote_copy(
                        src_ref=src,
                        dst_ref=dst,
                        send_sem=c_send,
                        recv_sem=c_recv.at[ch],
                        device_id=(to_seq, mp),
                        device_id_type=MESH,
                    ).start()

    wait_bytes(send_a.at[pl.ds(0, 7)], a_send)

    def out_copy(ch, a):
        lanes = pl.ds(256 * ch, 256)
        return pltpu.make_async_copy(
            send_a.at[a, :, lanes],
            out_hbm.at[pl.ds(pl.multiple_of(a * 512, 512), 512), lanes],
            out_sem.at[ch, a],
        )

    for ch in range(2):
        wait_bytes(recv_c.at[ch, :, pl.ds(0, 496)], c_recv.at[ch])
        wait_bytes(recv_c.at[ch, :, pl.ds(0, 16)], c_own.at[ch])

        @pl.loop(0, 8)
        def _(a):
            cut = slice(256 * ch, 256 * ch + 256)
            total = dot32(row_t[...], recv_c[ch, a])
            send_a[a, :, cut] = (xw[a, 16:, cut].astype(F32) + total).astype(BF16)
            out_copy(ch, a).start()

    for ch in range(2):

        @pl.loop(0, 8)
        def _(a):
            out_copy(ch, a).wait()

    halo.wait_send()
    wait_bytes(left_all.at[pl.ds(0, 7)], left_send)
    wait_bytes(recv_b.at[0, pl.ds(0, 255)], b_send)
    wait_bytes(recv_b.at[1, pl.ds(0, 255)], b_send)
    wait_bytes(recv_c.at[0, :, pl.ds(0, 496)], c_send)
    wait_bytes(recv_c.at[1, :, pl.ds(0, 496)], c_send)


def shards(
    activations,
    conv_weight,
    chan_right,
    chan_left,
    row_factor,
    col_factor,
    twiddle_one,
    twiddle_two,
    spectrum,
):
    any_space = pl.BlockSpec(memory_space=pl.ANY)
    vmem = pl.BlockSpec(memory_space=pltpu.VMEM)
    packed = chan_left.reshape(2, 4, 64, 64).transpose(1, 2, 0, 3).reshape(4, 64, 128)
    dma = pltpu.SemaphoreType.DMA
    scratch = [
        ((8, 528, 512), BF16),
        ((512, 64), BF16),
        ((4, 64, 128), BF16),
        ((8, 4, 64, 128), BF16),
        ((512, 512), BF16),
        ((512, 512), BF16),
        ((256, 256), BF16),
        ((256, 256), BF16),
        ((256, 256), BF16),
        ((512, 512), BF16),
        ((512, 512), BF16),
        ((4, 8, 128, 1024), BF16),
        ((16, 256, 128), F32),
        ((512, 512), BF16),
        ((8, 512, 512), BF16),
        ((8, 512, 512), BF16),
        ((4, 256, 1024), BF16),
        ((2, 8, 4, 128, 256), BF16),
        ((2, 256, 16, 256), BF16),
        ((16, 256, 256), BF16),
        ((2, 16, 256, 256), BF16),
        ((2, 256, 16, 256), BF16),
        ((2, 8, 512, 256), BF16),
    ]
    sems = [(6,), (8,), (8,), (), (), (), (), (), (2,), (), (), (2,), (2,), (), (2,), (2,), (2, 8)]
    return pl.pallas_call(
        kernel,
        name="monarch",
        out_shape=jax.ShapeDtypeStruct(activations.shape, activations.dtype),
        in_specs=[any_space, vmem, any_space, any_space, any_space, any_space, vmem, vmem, any_space],
        out_specs=any_space,
        scratch_shapes=[pltpu.VMEM(*one) for one in scratch]
        + [dma(shape) if shape else dma for shape in sems],
        compiler_params=pltpu.CompilerParams(
            collective_id=0, has_side_effects=True, vmem_limit_bytes=60 << 20
        ),
    )(
        activations,
        conv_weight,
        chan_right.reshape(512, 64),
        packed,
        row_factor,
        col_factor,
        twiddle_one.T,
        twiddle_two,
        spectrum,
    )


def solution(mesh):
    in_specs = (
        P("seq", "mp"),
        P(None, "mp"),
        P("mp", None, None),
        P("mp", None, None),
        P(),
        P(),
        P("seq", None),
        P(None, "seq"),
        P(None, "seq", "mp"),
    )
    out_specs = P("seq", "mp")
    return jax.shard_map(shards, mesh=mesh, in_specs=in_specs, out_specs=out_specs, check_vma=False)
```

```python
import jax
import jax.numpy as jnp
from jax import lax
from jax.experimental import pallas as pl
from jax.experimental.pallas import tpu as pltpu
from jax.sharding import PartitionSpec as P

MESH = pl.DeviceIdType.MESH
BF16 = jnp.bfloat16
F32 = jnp.float32


def dot32(a, b):
    return jnp.dot(a, b, preferred_element_type=F32)


def iota(shape, dim):
    return lax.broadcasted_iota(jnp.int32, shape, dim)


def one_hot(condition):
    return jnp.where(condition, 1.0, 0.0).astype(BF16)


def wait_bytes(ref, sem):
    pltpu.make_async_copy(ref, ref, sem).wait()


def kernel(
    x_hbm,
    taps,
    right_hbm,
    left_hbm,
    row_hbm,
    col_hbm,
    twiddle_one,
    twiddle_two,
    spectrum_hbm,
    out_hbm,
    xw,
    right,
    left_raw,
    left_own,
    left_all,
    row_n,
    row_f,
    row_t,
    col_f,
    col_t,
    swap,
    natural,
    right_w,
    left_w,
    twiddle_n,
    twiddle_a,
    twiddle_b,
    gated,
    send_a,
    recv_a,
    mixed,
    send_b,
    recv_b,
    columns,
    kernel_t,
    send_c,
    recv_c,
    ready,
    load_sem,
    row_sem,
    x_sem,
    tail_sem,
    halo_send,
    halo_recv,
    left_send,
    left_recv,
    a_send,
    a_recv,
    a_own,
    b_send,
    b_recv,
    b_own,
    c_send,
    c_recv,
    c_own,
    out_sem,
):
    seq, mp = lax.axis_index("seq"), lax.axis_index("mp")
    x, z_hi, core = seq // 8, seq // 2 % 4, seq % 2
    z_lo, y = mp // 4, mp % 4
    me = seq * 8 + mp

    def mp_peer(turn):
        return (z_lo + 1 + turn // 4) % 2 * 4 + (y + turn + 1) % 4

    barrier = pltpu.get_barrier_semaphore()

    @pl.loop(0, 7)
    def _(turn):
        peer = (seq, mp_peer(turn))
        pl.semaphore_signal(barrier, inc=1, device_id=peer, device_id_type=MESH)

    small = [
        pltpu.make_async_copy(src, dst, load_sem.at[i])
        for i, (src, dst) in enumerate(
            ((right_hbm, right), (row_hbm, row_n), (col_hbm, col_f), (left_hbm, left_raw))
        )
    ]
    for copy in small:
        copy.start()

    blocks = [(2, 0), (2, 1), (1, 0), (1, 1), (1, 2), (1, 3), (0, 0), (0, 1)]
    blocks += [(2, 2), (2, 3), (3, 0), (3, 1), (3, 2), (3, 3), (0, 2), (0, 3)]

    def block_rows(i):
        up, along = blocks[i]
        start = (x + along) % 4 * 128 + (z_hi + up) % 4 * 32
        return pl.ds(pl.multiple_of(start, 32), 32)

    row_copies = [
        pltpu.make_async_copy(row_hbm.at[block_rows(i)], row_f.at[pl.ds(32 * i, 32)], row_sem.at[i])
        for i in range(16)
    ]
    for copy in row_copies:
        copy.start()

    def x_copy(a):
        return pltpu.make_async_copy(
            x_hbm.at[pl.ds(pl.multiple_of(a * 512, 512), 512)],
            xw.at[a, pl.ds(16, 512)],
            x_sem.at[a],
        )

    def tail_copy(a):
        return pltpu.make_async_copy(
            x_hbm.at[pl.ds(pl.multiple_of(a * 512 - 16, 16), 16)],
            xw.at[a, pl.ds(0, 16)],
            tail_sem.at[a],
        )

    def front_row(step):
        return (y + 1 + step // 2) % 4 * 2 + step % 2

    @pl.loop(0, 8)
    def _(step):
        a = front_row(step)
        x_copy(a).start()

        @pl.when(a > 0)
        def _():
            tail_copy(a).start()

    kernel_copies = [
        pltpu.make_async_copy(
            spectrum_hbm.at[:, :, pl.ds(256 * ch, 256)], send_c.at[ch], load_sem.at[4 + ch]
        )
        for ch in range(2)
    ]
    for copy in kernel_copies:
        copy.start()

    @pl.loop(1, 32)
    def _(step):
        peer = ((seq + step) % 32, mp)
        pl.semaphore_signal(barrier, inc=1, device_id=peer, device_id_type=MESH)

    small[0].wait()
    col = iota((64, 512), 1)
    full = dot32(right[...], one_hot(iota((64, 512), 0) == col // 128 * 16 + col % 128 // 8))
    same = iota((512, 512), 0) // 64 == iota((512, 512), 1) % 8
    right_w[...] = jnp.where(same, full, 0.0).astype(BF16)
    for copy in small[1:] + row_copies:
        copy.wait()
    for kk in range(4):
        left_own[kk] = jnp.concatenate([left_raw[kk], left_raw[4 + kk]], 1)
    twiddle_n[...] = twiddle_one[...].T
    for i in range(16):
        twiddle_a[32 * i : 32 * i + 32] = twiddle_n[block_rows(i)]

    pl.semaphore_wait(barrier, 38)

    @pl.loop(0, 7)
    def _(turn):
        peer = (seq, mp_peer(turn))
        pl.semaphore_signal(ready, inc=1, device_id=peer, device_id_type=MESH)

    halo = pltpu.make_async_remote_copy(
        src_ref=x_hbm.at[pl.ds(4080, 16)],
        dst_ref=xw.at[0, pl.ds(0, 16)],
        send_sem=halo_send,
        recv_sem=halo_recv,
        device_id=((seq + 1) % 32, mp),
        device_id_type=MESH,
    )
    halo.start()

    def send_left():
        @pl.loop(0, 7)
        def _(turn):
            peer = mp_peer(turn)
            shift = jnp.where(turn < 4, jnp.where(z_lo == 1, 1, 3), 0)
            to_seq = (x * 4 + (z_hi + shift) % 4) * 2 + core
            pltpu.make_async_remote_copy(
                src_ref=left_own,
                dst_ref=left_all.at[mp],
                send_sem=left_send,
                recv_sem=left_recv,
                device_id=(to_seq, peer),
                device_id_type=MESH,
            ).start()

    def send_rows(step, part):
        a = front_row(step)

        def send(to_z):
            rows = pl.ds(pl.multiple_of((1 - to_z) * 256 + part * 64, 64), 64)
            pltpu.make_async_remote_copy(
                src_ref=send_a.at[a, rows],
                dst_ref=recv_a.at[mp, step % 2, pl.ds(part * 64, 64)],
                send_sem=a_send,
                recv_sem=a_recv.at[part],
                device_id=(seq, to_z * 4 + a // 2),
                device_id_type=MESH,
            ).start()

        send(1 - z_lo)

        @pl.when(step < 6)
        def _():
            send(z_lo)

    @pl.loop(0, 8)
    def _(step):
        a = front_row(step)
        x_copy(a).wait()

        @pl.when(a > 0)
        def _():
            tail_copy(a).wait()

        @pl.when(a == 0)
        def _():
            halo.wait_recv()

            @pl.when(seq == 0)
            def _():
                xw[0, pl.ds(0, 16)] = jnp.zeros((16, 512), BF16)

        @pl.loop(0, 4)
        def _(tile):
            start = pl.multiple_of(tile * 128, 128)
            window = xw[a, pl.ds(start, 144)].astype(F32)
            here = window[16:]
            conv_out = (
                taps[0:1] * here + taps[1:2] * window[15:143] + taps[2:3] * window[14:142]
            )
            gated[pl.ds(start, 128)] = (here * conv_out / (1.0 + jnp.exp(-conv_out))).astype(BF16)

        first = dot32(gated[...], right_w[...]).astype(BF16)
        scale = jnp.sum(jnp.where(iota((512, 8), 1) == a, twiddle_a[...], 0.0), 1, keepdims=True)
        send_a[a] = (dot32(row_f[...], first) * scale).astype(BF16)

        send_rows(step, 0)

        @pl.when(step == 1)
        def _():
            pl.semaphore_wait(ready, 7)
            send_left()

    own_rows = pltpu.make_async_copy(
        send_a.at[pl.ds(pl.multiple_of(2 * y, 2), 2), pl.ds(pl.multiple_of((1 - z_lo) * 256, 256), 256)],
        recv_a.at[mp],
        a_own,
    )
    own_rows.start()
    for part in range(1, 4):

        @pl.loop(0, 8)
        def _(step):
            send_rows(step, part)

    row_t[...] = row_n[...].astype(F32).T.astype(BF16)
    col_t[...] = col_f[...].astype(F32).T.astype(BF16)
    row, col = iota((256, 256), 0), iota((256, 256), 1)
    swap[...] = one_hot(row // 16 + row % 16 * 16 == col)
    row, col = iota((512, 512), 0), iota((512, 512), 1)
    natural[...] = one_hot(row // 16 % 8 * 64 + row // 128 * 16 + row % 16 == col)

    left_all[mp] = left_own[...]
    wait_bytes(left_all.at[pl.ds(0, 7)], left_recv)

    @pl.loop(0, 8)
    def _(owner):
        slab = left_all[owner].astype(F32).reshape(4, 8, 8, 128)
        slab = slab.swapaxes(0, 1).reshape(256, 128).astype(BF16)
        for u in range(2):
            spread = iota((128, 1024), 0) == iota((128, 1024), 1) // 16 + 64 * u
            full = dot32(slab, one_hot(spread))
            k = owner % 2 * 8 + 4 * u + iota((256, 1024), 0) // 8 % 4
            full = jnp.where(k == iota((256, 1024), 1) % 16, full, 0.0).astype(BF16)
            rows = pl.ds(pl.multiple_of((owner % 2 * 2 + u) * 32, 32), 32)
            left_w[owner // 2, :, rows] = full.reshape(8, 32, 1024)

    for ch in range(2):
        kernel_copies[ch].wait()

        @pl.loop(0, 16)
        def _(block):
            rows = pl.ds(pl.multiple_of(block * 16, 16), 16)
            turned = dot32(swap[...], send_c[ch, rows].reshape(256, 256)).astype(BF16)
            kernel_t[ch, :, rows] = turned.reshape(16, 16, 256)

    scales = twiddle_two[...].T
    for p in range(16):
        twiddle_b[p] = jnp.broadcast_to(scales[:, p : p + 1], (256, 128))

    own_rows.wait()

    first_a = pl.multiple_of(seq * 8 + y * 2, 2)

    def send_columns(ch, part, to_mp):
        up = [2, 3 - 2 * z_lo, 3 - 2 * z_lo, 0][part]
        along = [2 - 2 * z_lo, 0, 2, 2 - 2 * z_lo][part]

        @pl.loop(0, 4)
        def _(i):
            to_core = (core + i) % 2
            to_seq = ((x + along + i // 2) % 4 * 4 + (z_hi + up) % 4) * 2 + to_core
            rows = pl.ds(pl.multiple_of(part * 64 + i // 2 * 32 + to_core * 16, 16), 16)
            src = send_b.at[ch, to_mp, :, rows]
            dst = recv_b.at[ch, pl.ds(first_a, 2)]

            def remote():
                pltpu.make_async_remote_copy(
                    src_ref=src,
                    dst_ref=dst,
                    send_sem=b_send.at[ch],
                    recv_sem=b_recv.at[ch],
                    device_id=(to_seq, to_mp),
                    device_id_type=MESH,
                ).start()

            if part < 3:
                remote()
            else:
                own = jnp.logical_and(to_seq == seq, to_mp == mp)

                @pl.when(own)
                def _():
                    pltpu.make_async_copy(src, dst, b_own.at[ch]).start()

                @pl.when(jnp.logical_not(own))
                def _():
                    remote()

    for part in range(4):
        wait_bytes(recv_a.at[pl.ds(0, 7), :, pl.ds(0, 64)], a_recv.at[part])

        @pl.loop(0, 4)
        def _(group):
            lanes = pl.ds(pl.multiple_of(group * 128, 128), 128)
            block = jnp.concatenate(
                [
                    recv_a[m, :, 64 * part : 64 * part + 64, lanes].reshape(128, 128)
                    for m in range(8)
                ],
                1,
            )
            for n in range(4):
                cut = slice(256 * n, 256 * n + 256)
                weights = left_w[group, :, :, cut].reshape(1024, 256)
                mixed[group, :, cut] = dot32(block, weights).astype(BF16)

        @pl.loop(0, 8)
        def _(turn):
            to_mp = mp_peer(turn)
            lanes = pl.ds(pl.multiple_of(to_mp * 128, 128), 128)
            block = jnp.concatenate([mixed[group, :, lanes] for group in range(4)], 1)
            for ch in range(2):
                cut = slice(256 * ch, 256 * ch + 256)
                turned = dot32(block, natural[:, cut]).astype(BF16)
                send_b[ch, to_mp, :, 64 * part : 64 * part + 64] = turned.reshape(2, 64, 256)
            send_columns(0, part, to_mp)

        for late in {0: [0], 3: [1, 2, 3]}.get(part, []):

            @pl.loop(0, 8)
            def _(turn):
                send_columns(1, late, mp_peer(turn))

    for ch in range(2):
        @pl.when(z_lo == 1)
        def _():
            wait_bytes(recv_b.at[ch, pl.ds(0, 254)], b_recv.at[ch])
            wait_bytes(recv_b.at[ch, pl.ds(0, 2)], b_own.at[ch])

        @pl.when(z_lo == 0)
        def _():
            wait_bytes(recv_b.at[ch], b_recv.at[ch])


        @pl.loop(0, 16)
        def _(block):
            rows = pl.ds(pl.multiple_of(block * 16, 16), 16)
            turned = dot32(swap[...], recv_b[ch, rows].reshape(256, 256)).astype(BF16)
            columns[:, rows] = turned.reshape(16, 16, 256)

        @pl.loop(0, 16)
        def _(p):
            spectral = (dot32(col_f[...], columns[p]) * kernel_t[ch, p].astype(F32)).astype(BF16)
            back = dot32(col_t[...], spectral)
            scale = twiddle_b[p]
            columns[p] = (back * jnp.concatenate([scale, scale], 1)).astype(BF16)

        @pl.loop(0, 16)
        def _(i):
            block = (seq // 2 + i) % 16
            rows = pl.ds(pl.multiple_of(block * 16, 16), 16)
            turned = dot32(swap[...], columns[:, rows].reshape(256, 256)).astype(BF16)
            send_c[ch, rows] = turned.reshape(16, 16, 256)
            for to_core in range(2):
                to_seq = block * 2 + to_core
                src = send_c.at[ch, pl.ds(pl.multiple_of(to_seq * 8, 8), 8)]
                dst = recv_c.at[ch, :, pl.ds(pl.multiple_of(seq * 16, 16), 16)]

                @pl.when(to_seq == seq)
                def _(src=src, dst=dst):
                    pltpu.make_async_copy(src, dst, c_own.at[ch]).start()

                @pl.when(to_seq != seq)
                def _(src=src, dst=dst, to_seq=to_seq):
                    pltpu.make_async_remote_copy(
                        src_ref=src,
                        dst_ref=dst,
                        send_sem=c_send,
                        recv_sem=c_recv.at[ch],
                        device_id=(to_seq, mp),
                        device_id_type=MESH,
                    ).start()

    wait_bytes(recv_a.at[pl.ds(0, 7)], a_send)

    def out_copy(ch, a):
        lanes = pl.ds(256 * ch, 256)
        return pltpu.make_async_copy(
            send_a.at[a, :, lanes],
            out_hbm.at[pl.ds(pl.multiple_of(a * 512, 512), 512), lanes],
            out_sem.at[ch, a],
        )

    for ch in range(2):
        wait_bytes(recv_c.at[ch, :, pl.ds(0, 496)], c_recv.at[ch])
        wait_bytes(recv_c.at[ch, :, pl.ds(0, 16)], c_own.at[ch])

        @pl.loop(0, 8)
        def _(a):
            cut = slice(256 * ch, 256 * ch + 256)
            total = dot32(row_t[...], recv_c[ch, a])
            send_a[a, :, cut] = (xw[a, 16:, cut].astype(F32) + total).astype(BF16)
            out_copy(ch, a).start()

    for ch in range(2):

        @pl.loop(0, 8)
        def _(a):
            out_copy(ch, a).wait()

    halo.wait_send()
    wait_bytes(left_all.at[pl.ds(0, 7)], left_send)
    for ch in range(2):

        @pl.when(z_lo == 1)
        def _():
            wait_bytes(recv_b.at[ch, pl.ds(0, 254)], b_send.at[ch])

        @pl.when(z_lo == 0)
        def _():
            wait_bytes(recv_b.at[ch], b_send.at[ch])

    wait_bytes(recv_c.at[0, :, pl.ds(0, 496)], c_send)
    wait_bytes(recv_c.at[1, :, pl.ds(0, 496)], c_send)


def shards(
    activations,
    conv_weight,
    chan_right,
    chan_left,
    row_factor,
    col_factor,
    twiddle_one,
    twiddle_two,
    spectrum,
):
    any_space = pl.BlockSpec(memory_space=pl.ANY)
    vmem = pl.BlockSpec(memory_space=pltpu.VMEM)
    dma = pltpu.SemaphoreType.DMA
    scratch = [
        ((8, 528, 512), BF16),
        ((512, 64), BF16),
        ((8, 64, 64), BF16),
        ((4, 64, 128), BF16),
        ((8, 4, 64, 128), BF16),
        ((512, 512), BF16),
        ((512, 512), BF16),
        ((512, 512), BF16),
        ((256, 256), BF16),
        ((256, 256), BF16),
        ((256, 256), BF16),
        ((512, 512), BF16),
        ((512, 512), BF16),
        ((4, 8, 128, 1024), BF16),
        ((512, 8), F32),
        ((512, 8), F32),
        ((16, 256, 128), F32),
        ((512, 512), BF16),
        ((8, 512, 512), BF16),
        ((8, 2, 256, 512), BF16),
        ((4, 128, 1024), BF16),
        ((2, 8, 2, 256, 256), BF16),
        ((2, 256, 16, 256), BF16),
        ((16, 256, 256), BF16),
        ((2, 16, 256, 256), BF16),
        ((2, 256, 16, 256), BF16),
        ((2, 8, 512, 256), BF16),
    ]
    sems = [(6,), (16,), (8,), (8,), (), (), (), (), (), (4,), (), (2,), (2,), (2,), (), (2,), (2,), (2, 8)]
    return pl.pallas_call(
        kernel,
        name="monarch",
        out_shape=jax.ShapeDtypeStruct(activations.shape, activations.dtype),
        in_specs=[any_space, vmem, any_space, any_space, any_space, any_space, vmem, vmem, any_space],
        out_specs=any_space,
        scratch_shapes=[pltpu.VMEM(*one) for one in scratch]
        + [pltpu.SemaphoreType.REGULAR]
        + [dma(shape) if shape else dma for shape in sems],
        compiler_params=pltpu.CompilerParams(
            collective_id=0, has_side_effects=True, vmem_limit_bytes=60 << 20
        ),
    )(
        activations,
        conv_weight,
        chan_right.reshape(512, 64),
        chan_left,
        row_factor,
        col_factor,
        twiddle_one,
        twiddle_two.T,
        spectrum,
    )


def solution(mesh):
    in_specs = (
        P("seq", "mp"),
        P(None, "mp"),
        P("mp", None, None),
        P("mp", None, None),
        P(),
        P(),
        P("seq", None),
        P(None, "seq"),
        P(None, "seq", "mp"),
    )
    out_specs = P("seq", "mp")
    return jax.shard_map(shards, mesh=mesh, in_specs=in_specs, out_specs=out_specs, check_vma=False)
```

```python
import jax
import jax.numpy as jnp
from jax import lax
from jax.experimental import pallas as pl
from jax.experimental.pallas import tpu as pltpu
from jax.sharding import PartitionSpec as P

MESH = pl.DeviceIdType.MESH
BF16 = jnp.bfloat16
F32 = jnp.float32


def dot32(a, b):
    return jnp.dot(a, b, preferred_element_type=F32)


def iota(shape, dim):
    return lax.broadcasted_iota(jnp.int32, shape, dim)


def one_hot(condition):
    return jnp.where(condition, 1.0, 0.0).astype(BF16)


def column(table, index):
    return jnp.sum(jnp.where(iota(table.shape, 1) == index, table, 0.0), 1, keepdims=True)


def wait_bytes(ref, sem):
    pltpu.make_async_copy(ref, ref, sem).wait()


def kernel(
    x_hbm,
    taps_hbm,
    right_hbm,
    left_hbm,
    row_hbm,
    col_hbm,
    one_hbm,
    two_hbm,
    spectrum_hbm,
    out_hbm,
    xw,
    taps,
    twiddle_one,
    twiddle_two,
    right,
    left_raw,
    left_own,
    left_all,
    row_t,
    row_f,
    col_f,
    col_t,
    swap,
    natural,
    right_w,
    left_w,
    twiddle_n,
    twiddle_a,
    twiddle_c,
    send_a,
    recv_a,
    mixed,
    send_b,
    recv_b,
    columns,
    kernel_t,
    send_c,
    recv_c,
    ready,
    load_sem,
    row_sem,
    x_sem,
    tail_sem,
    halo_send,
    halo_recv,
    left_send,
    left_recv,
    pair_send,
    pair_recv,
    a_send,
    a_recv,
    a_own,
    b_send,
    b_recv,
    b_own,
    c_send,
    c_recv,
    c_own,
    out_sem,
):
    seq, mp = lax.axis_index("seq"), lax.axis_index("mp")
    x, z_hi, core = seq // 8, seq // 2 % 4, seq % 2
    z_lo, y = mp // 4, mp % 4
    me = seq * 8 + mp

    def mp_peer(turn):
        return (z_lo + 1 + turn // 4) % 2 * 4 + (y + turn + 1) % 4

    barrier = pltpu.get_barrier_semaphore()

    @pl.loop(0, 7)
    def _(turn):
        peer = (seq, mp_peer(turn))
        pl.semaphore_signal(barrier, inc=1, device_id=peer, device_id_type=MESH)

    small = [
        pltpu.make_async_copy(src, dst, load_sem.at[i])
        for i, (src, dst) in enumerate(
            (
                (right_hbm, right),
                (row_hbm, row_t),
                (col_hbm, col_f),
                (left_hbm, left_raw),
                (taps_hbm, taps),
                (one_hbm, twiddle_one),
                (two_hbm, twiddle_two),
            )
        )
    ]
    for copy in small:
        copy.start()

    upper = [(1, 0), (2, 0), (1, 1), (0, 0), (1, 2), (2, 1), (1, 3), (0, 1)]
    lower = [(3, 0), (2, 2), (3, 1), (0, 2), (3, 2), (2, 3), (3, 3), (0, 3)]
    blocks = upper + lower

    def block_rows(i):
        up, along = blocks[i]
        start = (x + along) % 4 * 128 + (z_hi + up) % 4 * 32
        return pl.ds(pl.multiple_of(start, 32), 32)

    row_copies = [
        pltpu.make_async_copy(row_hbm.at[block_rows(i)], row_f.at[pl.ds(32 * i, 32)], row_sem.at[i])
        for i in range(16)
    ]
    for copy in row_copies:
        copy.start()

    def x_copy(a):
        return pltpu.make_async_copy(
            x_hbm.at[pl.ds(pl.multiple_of(a * 512, 512), 512)],
            xw.at[a, pl.ds(16, 512)],
            x_sem.at[a],
        )

    def tail_copy(a):
        return pltpu.make_async_copy(
            x_hbm.at[pl.ds(pl.multiple_of(a * 512 - 16, 16), 16)],
            xw.at[a, pl.ds(0, 16)],
            tail_sem.at[a],
        )

    def front_row(step):
        return (y + 1 + step // 2) % 4 * 2 + 1 - step % 2

    @pl.loop(0, 8)
    def _(step):
        a = front_row(step)
        x_copy(a).start()

        @pl.when(a > 0)
        def _():
            tail_copy(a).start()

    kernel_copies = [
        pltpu.make_async_copy(
            spectrum_hbm.at[:, :, pl.ds(256 * ch, 256)], send_c.at[ch], load_sem.at[7 + ch]
        )
        for ch in range(2)
    ]
    for copy in kernel_copies:
        copy.start()

    @pl.loop(1, 32)
    def _(step):
        peer = ((seq + step) % 32, mp)
        pl.semaphore_signal(barrier, inc=1, device_id=peer, device_id_type=MESH)

    small[0].wait()
    col = iota((64, 512), 1)
    full = dot32(right[...], one_hot(iota((64, 512), 0) == col // 128 * 16 + col % 128 // 8))
    same = iota((512, 512), 0) // 64 == iota((512, 512), 1) % 8
    right_w[...] = jnp.where(same, full, 0.0).astype(BF16)
    for copy in small[1:] + row_copies:
        copy.wait()
    for kk in range(4):
        left_own[kk] = jnp.concatenate([left_raw[kk], left_raw[4 + kk]], 1)
    twiddle_n[...] = twiddle_one[...].T
    for i in range(16):
        twiddle_a[32 * i : 32 * i + 32] = twiddle_n[block_rows(i)]

    halo = pltpu.make_async_remote_copy(
        src_ref=x_hbm.at[pl.ds(4080, 16)],
        dst_ref=xw.at[0, pl.ds(0, 16)],
        send_sem=halo_send,
        recv_sem=halo_recv,
        device_id=((seq + 1) % 32, mp),
        device_id_type=MESH,
    )

    def send_left():
        @pl.loop(0, 7)
        def _(turn):
            peer = mp_peer(turn)
            shift = jnp.where(turn < 4, jnp.where(z_lo == 1, 1, 3), 0)
            to_seq = (x * 4 + (z_hi + shift) % 4) * 2 + core
            pltpu.make_async_remote_copy(
                src_ref=left_own.at[pl.ds(core * 2, 2)],
                dst_ref=left_all.at[mp, pl.ds(core * 2, 2)],
                send_sem=left_send,
                recv_sem=left_recv,
                device_id=(to_seq, peer),
                device_id_type=MESH,
            ).start()

    def send_rows(step, part):
        a = front_row(step)

        def send(to_z):
            rows = pl.ds(pl.multiple_of((1 - to_z) * 256 + part * 64, 64), 64)
            pltpu.make_async_remote_copy(
                src_ref=send_a.at[a, rows],
                dst_ref=recv_a.at[mp, a % 2, pl.ds(part * 64, 64)],
                send_sem=a_send,
                recv_sem=a_recv.at[part],
                device_id=(seq, to_z * 4 + a // 2),
                device_id_type=MESH,
            ).start()

        send(1 - z_lo)

        @pl.when(step < 6)
        def _():
            send(z_lo)

    def front(a):
        x_copy(a).wait()

        @pl.when(a > 0)
        def _():
            tail_copy(a).wait()

        @pl.when(a == 0)
        def _():
            halo.wait_recv()

            @pl.when(seq == 0)
            def _():
                xw[0, pl.ds(0, 16)] = jnp.zeros((16, 512), BF16)

        @pl.loop(0, 4)
        def _(tile):
            start = pl.multiple_of(tile * 128, 128)
            window = xw[a, pl.ds(start, 144)].astype(F32)
            here = window[16:]
            conv_out = (
                taps[0:1] * here + taps[1:2] * window[15:143] + taps[2:3] * window[14:142]
            )
            mixed[pl.ds(start, 128), :512] = (here * conv_out / (1.0 + jnp.exp(-conv_out))).astype(BF16)

        first = dot32(mixed[:, :512], right_w[...]).astype(BF16)
        send_a[a] = (dot32(row_f[...], first) * column(twiddle_a[...], a)).astype(BF16)

    front(front_row(0))

    pl.semaphore_wait(barrier, 38)

    @pl.loop(0, 7)
    def _(turn):
        peer = (seq, mp_peer(turn))
        pl.semaphore_signal(ready, inc=1, device_id=peer, device_id_type=MESH)

    halo.start()
    send_rows(0, 0)
    pl.semaphore_wait(ready, 7)
    send_left()

    @pl.loop(1, 8)
    def _(step):
        front(front_row(step))
        send_rows(step, 0)

    own_rows = pltpu.make_async_copy(
        send_a.at[pl.ds(pl.multiple_of(2 * y, 2), 2), pl.ds(pl.multiple_of((1 - z_lo) * 256, 256), 256)],
        recv_a.at[mp],
        a_own,
    )
    own_rows.start()
    for part in range(1, 4):

        @pl.loop(0, 8)
        def _(step):
            send_rows(step, part)

    row_t[...] = row_t[...].astype(F32).T.astype(BF16)
    col_t[...] = col_f[...].astype(F32).T.astype(BF16)
    row, col = iota((256, 256), 0), iota((256, 256), 1)
    swap[...] = one_hot(row // 16 + row % 16 * 16 == col)
    row, col = iota((512, 512), 0), iota((512, 512), 1)
    natural[...] = one_hot(row // 16 % 8 * 64 + row // 128 * 16 + row % 16 == col)

    halves = left_all.at[:, pl.ds(core * 2, 2)]
    left_all[mp, pl.ds(core * 2, 2)] = left_own[pl.ds(core * 2, 2)]
    wait_bytes(left_all.at[pl.ds(0, 7), pl.ds(0, 2)], left_recv)
    to_pair = pltpu.make_async_remote_copy(
        src_ref=halves,
        dst_ref=halves,
        send_sem=pair_send,
        recv_sem=pair_recv,
        device_id=(seq + 1 - 2 * core, mp),
        device_id_type=MESH,
    )
    to_pair.start()
    to_pair.wait_recv()

    @pl.loop(0, 8)
    def _(owner):
        slab = left_all[owner].astype(F32).reshape(4, 8, 8, 128)
        slab = slab.swapaxes(0, 1).reshape(256, 128).astype(BF16)
        for u in range(2):
            spread = iota((128, 1024), 0) == iota((128, 1024), 1) // 16 + 64 * u
            full = dot32(slab, one_hot(spread))
            k = owner % 2 * 8 + 4 * u + iota((256, 1024), 0) // 8 % 4
            full = jnp.where(k == iota((256, 1024), 1) % 16, full, 0.0).astype(BF16)
            rows = pl.ds(pl.multiple_of((owner % 2 * 2 + u) * 32, 32), 32)
            left_w[owner // 2, :, rows] = full.reshape(8, 32, 1024)

    for ch in range(2):
        kernel_copies[ch].wait()

        @pl.loop(0, 16)
        def _(block):
            rows = pl.ds(pl.multiple_of(block * 16, 16), 16)
            turned = dot32(swap[...], send_c[ch, rows].reshape(256, 256)).astype(BF16)
            kernel_t[ch, :, rows] = turned.reshape(16, 16, 256)

    twiddle_c[...] = twiddle_two[...].T

    own_rows.wait()

    first_a = pl.multiple_of(seq * 8 + y * 2, 2)

    def send_columns(ch, part, to_mp):
        def steps(k, i):
            high = jnp.where(i // 2 == 0, upper[2 * part][k], upper[2 * part + 1][k])
            low = jnp.where(i // 2 == 0, lower[2 * part][k], lower[2 * part + 1][k])
            return jnp.where(z_lo == 1, high, low)

        @pl.loop(0, 4)
        def _(i):
            to_core = (core + i) % 2
            to_seq = ((x + steps(1, i)) % 4 * 4 + (z_hi + steps(0, i)) % 4) * 2 + to_core
            rows = pl.ds(pl.multiple_of(part * 64 + i // 2 * 32 + to_core * 16, 16), 16)
            src = send_b.at[ch, to_mp, :, rows]
            dst = recv_b.at[ch, pl.ds(first_a, 2)]

            def remote():
                pltpu.make_async_remote_copy(
                    src_ref=src,
                    dst_ref=dst,
                    send_sem=b_send.at[ch],
                    recv_sem=b_recv.at[ch],
                    device_id=(to_seq, to_mp),
                    device_id_type=MESH,
                ).start()

            if (0, 0) not in upper[2 * part : 2 * part + 2]:
                remote()
            else:
                own = jnp.logical_and(to_seq == seq, to_mp == mp)

                @pl.when(own)
                def _():
                    pltpu.make_async_copy(src, dst, b_own.at[ch]).start()

                @pl.when(jnp.logical_not(own))
                def _():
                    remote()

    for part in range(4):
        wait_bytes(recv_a.at[pl.ds(0, 7), :, pl.ds(0, 64)], a_recv.at[part])

        @pl.loop(0, 4)
        def _(group):
            lanes = pl.ds(pl.multiple_of(group * 128, 128), 128)
            block = jnp.concatenate(
                [
                    recv_a[m, :, 64 * part : 64 * part + 64, lanes].reshape(128, 128)
                    for m in range(8)
                ],
                1,
            )
            rows = pl.ds(pl.multiple_of(group * 128, 128), 128)
            for n in range(4):
                cut = slice(256 * n, 256 * n + 256)
                weights = left_w[group, :, :, cut].reshape(1024, 256)
                mixed[rows, cut] = dot32(block, weights).astype(BF16)

        @pl.loop(0, 8)
        def _(turn):
            to_mp = mp_peer(turn)
            lanes = pl.ds(pl.multiple_of(to_mp * 128, 128), 128)
            block = jnp.concatenate([mixed[128 * group : 128 * group + 128, lanes] for group in range(4)], 1)
            for ch in range(2):
                cut = slice(256 * ch, 256 * ch + 256)
                turned = dot32(block, natural[:, cut]).astype(BF16)
                send_b[ch, to_mp, :, 64 * part : 64 * part + 64] = turned.reshape(2, 64, 256)
            send_columns(0, part, to_mp)

        for late in {0: [0], 3: [1, 2, 3]}.get(part, []):

            @pl.loop(0, 8)
            def _(turn):
                send_columns(1, late, mp_peer(turn))

    for ch in range(2):
        @pl.when(z_lo == 1)
        def _():
            wait_bytes(recv_b.at[ch, pl.ds(0, 254)], b_recv.at[ch])
            wait_bytes(recv_b.at[ch, pl.ds(0, 2)], b_own.at[ch])

        @pl.when(z_lo == 0)
        def _():
            wait_bytes(recv_b.at[ch], b_recv.at[ch])


        @pl.loop(0, 16)
        def _(block):
            rows = pl.ds(pl.multiple_of(block * 16, 16), 16)
            turned = dot32(swap[...], recv_b[ch, rows].reshape(256, 256)).astype(BF16)
            columns[:, rows] = turned.reshape(16, 16, 256)

        @pl.loop(0, 16)
        def _(p):
            spectral = (dot32(col_f[...], columns[p]) * kernel_t[ch, p].astype(F32)).astype(BF16)
            back = dot32(col_t[...], spectral)
            columns[p] = (back * column(twiddle_c[...], p)).astype(BF16)

        @pl.loop(0, 16)
        def _(i):
            block = (seq // 2 + i) % 16
            rows = pl.ds(pl.multiple_of(block * 16, 16), 16)
            turned = dot32(swap[...], columns[:, rows].reshape(256, 256)).astype(BF16)
            send_c[ch, rows] = turned.reshape(16, 16, 256)
            for to_core in range(2):
                to_seq = block * 2 + to_core
                src = send_c.at[ch, pl.ds(pl.multiple_of(to_seq * 8, 8), 8)]
                dst = recv_c.at[ch, :, pl.ds(pl.multiple_of(seq * 16, 16), 16)]

                @pl.when(to_seq == seq)
                def _(src=src, dst=dst):
                    pltpu.make_async_copy(src, dst, c_own.at[ch]).start()

                @pl.when(to_seq != seq)
                def _(src=src, dst=dst, to_seq=to_seq):
                    pltpu.make_async_remote_copy(
                        src_ref=src,
                        dst_ref=dst,
                        send_sem=c_send,
                        recv_sem=c_recv.at[ch],
                        device_id=(to_seq, mp),
                        device_id_type=MESH,
                    ).start()

    wait_bytes(recv_a.at[pl.ds(0, 7)], a_send)

    def out_copy(ch, a):
        lanes = pl.ds(256 * ch, 256)
        return pltpu.make_async_copy(
            send_a.at[a, :, lanes],
            out_hbm.at[pl.ds(pl.multiple_of(a * 512, 512), 512), lanes],
            out_sem.at[ch, a],
        )


    for ch in range(2):
        wait_bytes(recv_c.at[ch, :, pl.ds(0, 496)], c_recv.at[ch])
        wait_bytes(recv_c.at[ch, :, pl.ds(0, 16)], c_own.at[ch])

        @pl.loop(0, 8)
        def _(a):
            cut = slice(256 * ch, 256 * ch + 256)
            total = dot32(row_t[...], recv_c[ch, a])
            send_a[a, :, cut] = (xw[a, 16:, cut].astype(F32) + total).astype(BF16)
            out_copy(ch, a).start()

    for ch in range(2):

        @pl.loop(0, 8)
        def _(a):
            out_copy(ch, a).wait()

    halo.wait_send()
    to_pair.wait_send()
    wait_bytes(left_all.at[pl.ds(0, 7), pl.ds(0, 2)], left_send)
    for ch in range(2):

        @pl.when(z_lo == 1)
        def _():
            wait_bytes(recv_b.at[ch, pl.ds(0, 254)], b_send.at[ch])

        @pl.when(z_lo == 0)
        def _():
            wait_bytes(recv_b.at[ch], b_send.at[ch])

    wait_bytes(recv_c.at[0, :, pl.ds(0, 496)], c_send)
    wait_bytes(recv_c.at[1, :, pl.ds(0, 496)], c_send)


def shards(
    activations,
    conv_weight,
    chan_right,
    chan_left,
    row_factor,
    col_factor,
    twiddle_one,
    twiddle_two,
    spectrum,
):
    hbm = pl.BlockSpec(memory_space=pltpu.HBM)
    dma = pltpu.SemaphoreType.DMA
    scratch = [
        ((8, 528, 512), BF16),
        ((3, 512), F32),
        ((8, 512), F32),
        ((16, 256), F32),
        ((512, 64), BF16),
        ((8, 64, 64), BF16),
        ((4, 64, 128), BF16),
        ((8, 4, 64, 128), BF16),
        ((512, 512), BF16),
        ((512, 512), BF16),
        ((256, 256), BF16),
        ((256, 256), BF16),
        ((256, 256), BF16),
        ((512, 512), BF16),
        ((512, 512), BF16),
        ((4, 8, 128, 1024), BF16),
        ((512, 8), F32),
        ((512, 8), F32),
        ((256, 16), F32),
        ((8, 512, 512), BF16),
        ((8, 2, 256, 512), BF16),
        ((512, 1024), BF16),
        ((2, 8, 2, 256, 256), BF16),
        ((2, 256, 16, 256), BF16),
        ((16, 256, 256), BF16),
        ((2, 16, 256, 256), BF16),
        ((2, 256, 16, 256), BF16),
        ((2, 8, 512, 256), BF16),
    ]
    sems = [(9,), (16,), (8,), (8,), (), (), (), (), (), (), (), (4,), (), (2,), (2,), (2,), (), (2,), (2,), (2, 8)]
    return pl.pallas_call(
        kernel,
        name="monarch",
        out_shape=jax.ShapeDtypeStruct(activations.shape, activations.dtype),
        in_specs=[hbm] * 9,
        out_specs=hbm,
        scratch_shapes=[pltpu.VMEM(*one) for one in scratch]
        + [pltpu.SemaphoreType.REGULAR]
        + [dma(shape) if shape else dma for shape in sems],
        compiler_params=pltpu.CompilerParams(
            collective_id=0, has_side_effects=True, vmem_limit_bytes=60 << 20
        ),
    )(
        activations,
        conv_weight,
        chan_right.reshape(512, 64),
        chan_left,
        row_factor,
        col_factor,
        twiddle_one,
        twiddle_two.T,
        spectrum,
    )


def solution(mesh):
    in_specs = (
        P("seq", "mp"),
        P(None, "mp"),
        P("mp", None, None),
        P("mp", None, None),
        P(),
        P(),
        P("seq", None),
        P(None, "seq"),
        P(None, "seq", "mp"),
    )
    out_specs = P("seq", "mp")
    return jax.shard_map(shards, mesh=mesh, in_specs=in_specs, out_specs=out_specs, check_vma=False)
```

```python
import jax
import jax.numpy as jnp
from jax import lax
from jax.experimental import pallas as pl
from jax.experimental.pallas import tpu as pltpu
from jax.sharding import PartitionSpec as P

MESH = pl.DeviceIdType.MESH
BF16 = jnp.bfloat16
F32 = jnp.float32


def dot32(a, b):
    return jnp.dot(a, b, preferred_element_type=F32)


def iota(shape, dim):
    return lax.broadcasted_iota(jnp.int32, shape, dim)


def one_hot(condition):
    return jnp.where(condition, 1.0, 0.0).astype(BF16)


def column(table, index):
    return jnp.sum(jnp.where(iota(table.shape, 1) == index, table, 0.0), 1, keepdims=True)


def wait_bytes(ref, sem):
    pltpu.make_async_copy(ref, ref, sem).wait()


def kernel(
    x_hbm,
    taps_hbm,
    right_hbm,
    left_hbm,
    row_hbm,
    col_hbm,
    one_hbm,
    two_hbm,
    spectrum_hbm,
    out_hbm,
    xw,
    taps,
    twiddle_one,
    twiddle_two,
    right,
    left_raw,
    left_own,
    left_all,
    row_t,
    row_f,
    col_f,
    col_t,
    swap,
    natural,
    right_w,
    left_w,
    twiddle_n,
    twiddle_a,
    twiddle_c,
    send_a,
    recv_a,
    mixed,
    send_b,
    recv_b,
    columns,
    kernel_t,
    send_c,
    recv_c,
    ready,
    load_sem,
    row_sem,
    x_sem,
    tail_sem,
    halo_send,
    halo_recv,
    left_send,
    left_recv,
    pair_send,
    pair_recv,
    a_send,
    a_recv,
    a_own,
    b_send,
    b_recv,
    b_own,
    c_send,
    c_recv,
    c_own,
    out_sem,
):
    seq, mp = lax.axis_index("seq"), lax.axis_index("mp")
    x, z_hi, core = seq // 8, seq // 2 % 4, seq % 2
    z_lo, y = mp // 4, mp % 4
    me = seq * 8 + mp

    def mp_peer(turn):
        return (z_lo + 1 + turn // 4) % 2 * 4 + (y + turn + 1) % 4

    barrier = pltpu.get_barrier_semaphore()

    @pl.loop(0, 7)
    def _(turn):
        peer = (seq, mp_peer(turn))
        pl.semaphore_signal(barrier, inc=1, device_id=peer, device_id_type=MESH)

    small = [
        pltpu.make_async_copy(src, dst, load_sem.at[i])
        for i, (src, dst) in enumerate(
            (
                (right_hbm, right),
                (row_hbm, row_t),
                (col_hbm, col_f),
                (left_hbm, left_raw),
                (taps_hbm, taps),
                (one_hbm, twiddle_one),
                (two_hbm, twiddle_two),
            )
        )
    ]
    for copy in small:
        copy.start()

    upper = [(1, 0), (2, 0), (1, 1), (0, 0), (1, 2), (2, 1), (1, 3), (0, 1)]
    lower = [(3, 0), (2, 2), (3, 1), (0, 2), (3, 2), (2, 3), (3, 3), (0, 3)]
    blocks = upper + lower

    def block_rows(i):
        up, along = blocks[i]
        start = (x + along) % 4 * 128 + (z_hi + up) % 4 * 32
        return pl.ds(pl.multiple_of(start, 32), 32)

    row_copies = [
        pltpu.make_async_copy(row_hbm.at[block_rows(i)], row_f.at[pl.ds(32 * i, 32)], row_sem.at[i])
        for i in range(16)
    ]
    for copy in row_copies:
        copy.start()

    def x_copy(a):
        return pltpu.make_async_copy(
            x_hbm.at[pl.ds(pl.multiple_of(a * 512, 512), 512)],
            xw.at[a, pl.ds(16, 512)],
            x_sem.at[a],
        )

    def tail_copy(a):
        return pltpu.make_async_copy(
            x_hbm.at[pl.ds(pl.multiple_of(a * 512 - 16, 16), 16)],
            xw.at[a, pl.ds(0, 16)],
            tail_sem.at[a],
        )

    def front_row(step):
        return (y + 1 + step // 2) % 4 * 2 + 1 - step % 2

    @pl.loop(0, 8)
    def _(step):
        a = front_row(step)
        x_copy(a).start()

        @pl.when(a > 0)
        def _():
            tail_copy(a).start()

    kernel_copies = [
        pltpu.make_async_copy(
            spectrum_hbm.at[:, :, pl.ds(256 * ch, 256)], send_c.at[ch], load_sem.at[7 + ch]
        )
        for ch in range(2)
    ]
    for copy in kernel_copies:
        copy.start()

    @pl.loop(1, 32)
    def _(step):
        peer = ((seq + step) % 32, mp)
        pl.semaphore_signal(barrier, inc=1, device_id=peer, device_id_type=MESH)

    small[0].wait()
    col = iota((64, 512), 1)
    full = dot32(right[...], one_hot(iota((64, 512), 0) == col // 128 * 16 + col % 128 // 8))
    same = iota((512, 512), 0) // 64 == iota((512, 512), 1) % 8
    right_w[...] = jnp.where(same, full, 0.0).astype(BF16)
    for copy in small[1:] + row_copies:
        copy.wait()
    for kk in range(4):
        left_own[kk] = jnp.concatenate([left_raw[kk], left_raw[4 + kk]], 1)
    twiddle_n[...] = twiddle_one[...].T
    for i in range(16):
        twiddle_a[32 * i : 32 * i + 32] = twiddle_n[block_rows(i)]

    halo = pltpu.make_async_remote_copy(
        src_ref=x_hbm.at[pl.ds(4080, 16)],
        dst_ref=xw.at[0, pl.ds(0, 16)],
        send_sem=halo_send,
        recv_sem=halo_recv,
        device_id=((seq + 1) % 32, mp),
        device_id_type=MESH,
    )

    def send_left():
        @pl.loop(0, 7)
        def _(turn):
            peer = mp_peer(turn)
            shift = jnp.where(turn < 4, jnp.where(z_lo == 1, 1, 3), 0)
            to_seq = (x * 4 + (z_hi + shift) % 4) * 2 + core
            pltpu.make_async_remote_copy(
                src_ref=left_own.at[pl.ds(core * 2, 2)],
                dst_ref=left_all.at[mp, pl.ds(core * 2, 2)],
                send_sem=left_send,
                recv_sem=left_recv,
                device_id=(to_seq, peer),
                device_id_type=MESH,
            ).start()

    def send_rows(step, part):
        a = front_row(step)

        def send(to_z):
            rows = pl.ds(pl.multiple_of((1 - to_z) * 256 + part * 64, 64), 64)
            pltpu.make_async_remote_copy(
                src_ref=send_a.at[a, rows],
                dst_ref=recv_a.at[mp, a % 2, pl.ds(part * 64, 64)],
                send_sem=a_send,
                recv_sem=a_recv.at[part],
                device_id=(seq, to_z * 4 + a // 2),
                device_id_type=MESH,
            ).start()

        send(1 - z_lo)

        @pl.when(step < 6)
        def _():
            send(z_lo)

    def front(a):
        x_copy(a).wait()

        @pl.when(a > 0)
        def _():
            tail_copy(a).wait()

        @pl.when(a == 0)
        def _():
            halo.wait_recv()

            @pl.when(seq == 0)
            def _():
                xw[0, pl.ds(0, 16)] = jnp.zeros((16, 512), BF16)

        @pl.loop(0, 4)
        def _(tile):
            start = pl.multiple_of(tile * 128, 128)
            window = xw[a, pl.ds(start, 144)].astype(F32)
            here = window[16:]
            conv_out = (
                taps[0:1] * here + taps[1:2] * window[15:143] + taps[2:3] * window[14:142]
            )
            mixed[pl.ds(start, 128), :512] = (here * conv_out / (1.0 + jnp.exp(-conv_out))).astype(BF16)

        first = dot32(mixed[:, :512], right_w[...]).astype(BF16)
        send_a[a] = (dot32(row_f[...], first) * column(twiddle_a[...], a)).astype(BF16)

    front(front_row(0))

    pl.semaphore_wait(barrier, 38)

    @pl.loop(0, 7)
    def _(turn):
        peer = (seq, mp_peer(turn))
        pl.semaphore_signal(ready, inc=1, device_id=peer, device_id_type=MESH)

    halo.start()
    send_rows(0, 0)
    pl.semaphore_wait(ready, 7)
    send_left()

    @pl.loop(1, 8)
    def _(step):
        front(front_row(step))
        send_rows(step, 0)

    own_rows = pltpu.make_async_copy(
        send_a.at[pl.ds(pl.multiple_of(2 * y, 2), 2), pl.ds(pl.multiple_of((1 - z_lo) * 256, 256), 256)],
        recv_a.at[mp],
        a_own,
    )
    own_rows.start()
    for part in range(1, 4):

        @pl.loop(0, 8)
        def _(step):
            send_rows(step, part)

    row_t[...] = row_t[...].astype(F32).T.astype(BF16)
    col_t[...] = col_f[...].astype(F32).T.astype(BF16)
    row, col = iota((256, 256), 0), iota((256, 256), 1)
    swap[...] = one_hot(row // 16 + row % 16 * 16 == col)
    row, col = iota((512, 512), 0), iota((512, 512), 1)
    natural[...] = one_hot(row // 16 % 8 * 64 + row // 128 * 16 + row % 16 == col)

    halves = left_all.at[:, pl.ds(core * 2, 2)]
    left_all[mp, pl.ds(core * 2, 2)] = left_own[pl.ds(core * 2, 2)]
    wait_bytes(left_all.at[pl.ds(0, 7), pl.ds(0, 2)], left_recv)
    to_pair = pltpu.make_async_remote_copy(
        src_ref=halves,
        dst_ref=halves,
        send_sem=pair_send,
        recv_sem=pair_recv,
        device_id=(seq + 1 - 2 * core, mp),
        device_id_type=MESH,
    )
    to_pair.start()
    to_pair.wait_recv()

    @pl.loop(0, 8)
    def _(owner):
        slab = left_all[owner].astype(F32).reshape(4, 8, 8, 128)
        slab = slab.swapaxes(0, 1).reshape(256, 128).astype(BF16)
        for u in range(2):
            spread = iota((128, 1024), 0) == iota((128, 1024), 1) // 16 + 64 * u
            full = dot32(slab, one_hot(spread))
            k = owner % 2 * 8 + 4 * u + iota((256, 1024), 0) // 8 % 4
            full = jnp.where(k == iota((256, 1024), 1) % 16, full, 0.0).astype(BF16)
            rows = pl.ds(pl.multiple_of((owner % 2 * 2 + u) * 32, 32), 32)
            left_w[owner // 2, :, rows] = full.reshape(8, 32, 1024)

    for ch in range(2):
        kernel_copies[ch].wait()

        @pl.loop(0, 16)
        def _(block):
            rows = pl.ds(pl.multiple_of(block * 16, 16), 16)
            turned = dot32(swap[...], send_c[ch, rows].reshape(256, 256)).astype(BF16)
            kernel_t[ch, :, rows] = turned.reshape(16, 16, 256)

    twiddle_c[...] = twiddle_two[...].T

    own_rows.wait()

    first_a = pl.multiple_of(seq * 8 + y * 2, 2)

    def send_columns(ch, part, to_mp):
        def steps(k, i):
            high = jnp.where(i // 2 == 0, upper[2 * part][k], upper[2 * part + 1][k])
            low = jnp.where(i // 2 == 0, lower[2 * part][k], lower[2 * part + 1][k])
            return jnp.where(z_lo == 1, high, low)

        @pl.loop(0, 4)
        def _(i):
            to_core = (core + i) % 2
            to_seq = ((x + steps(1, i)) % 4 * 4 + (z_hi + steps(0, i)) % 4) * 2 + to_core
            rows = pl.ds(pl.multiple_of(part * 64 + i // 2 * 32 + to_core * 16, 16), 16)
            src = send_b.at[ch, to_mp, :, rows]
            dst = recv_b.at[ch, pl.ds(first_a, 2)]

            def remote():
                pltpu.make_async_remote_copy(
                    src_ref=src,
                    dst_ref=dst,
                    send_sem=b_send.at[ch],
                    recv_sem=b_recv.at[ch],
                    device_id=(to_seq, to_mp),
                    device_id_type=MESH,
                ).start()

            if (0, 0) not in upper[2 * part : 2 * part + 2]:
                remote()
            else:
                own = jnp.logical_and(to_seq == seq, to_mp == mp)

                @pl.when(own)
                def _():
                    pltpu.make_async_copy(src, dst, b_own.at[ch]).start()

                @pl.when(jnp.logical_not(own))
                def _():
                    remote()

    for part in range(4):
        wait_bytes(recv_a.at[pl.ds(0, 7), :, pl.ds(0, 64)], a_recv.at[part])

        @pl.loop(0, 4)
        def _(group):
            lanes = pl.ds(pl.multiple_of(group * 128, 128), 128)
            block = jnp.concatenate(
                [
                    recv_a[m, :, 64 * part : 64 * part + 64, lanes].reshape(128, 128)
                    for m in range(8)
                ],
                1,
            )
            rows = pl.ds(pl.multiple_of(group * 128, 128), 128)
            for n in range(4):
                cut = slice(256 * n, 256 * n + 256)
                weights = left_w[group, :, :, cut].reshape(1024, 256)
                mixed[rows, cut] = dot32(block, weights).astype(BF16)

        @pl.loop(0, 8)
        def _(turn):
            to_mp = mp_peer(turn)
            lanes = pl.ds(pl.multiple_of(to_mp * 128, 128), 128)
            block = jnp.concatenate([mixed[128 * group : 128 * group + 128, lanes] for group in range(4)], 1)
            for ch in range(2):
                cut = slice(256 * ch, 256 * ch + 256)
                turned = dot32(block, natural[:, cut]).astype(BF16)
                send_b[ch, to_mp, :, 64 * part : 64 * part + 64] = turned.reshape(2, 64, 256)
            send_columns(0, part, to_mp)

        for late in {3: [0, 1, 2, 3]}.get(part, []):

            @pl.loop(0, 8)
            def _(turn):
                send_columns(1, late, mp_peer(turn))

    for ch in range(2):
        @pl.when(z_lo == 1)
        def _():
            wait_bytes(recv_b.at[ch, pl.ds(0, 254)], b_recv.at[ch])
            wait_bytes(recv_b.at[ch, pl.ds(0, 2)], b_own.at[ch])

        @pl.when(z_lo == 0)
        def _():
            wait_bytes(recv_b.at[ch], b_recv.at[ch])


        @pl.loop(0, 16)
        def _(block):
            rows = pl.ds(pl.multiple_of(block * 16, 16), 16)
            turned = dot32(swap[...], recv_b[ch, rows].reshape(256, 256)).astype(BF16)
            columns[:, rows] = turned.reshape(16, 16, 256)

        @pl.loop(0, 16)
        def _(p):
            spectral = (dot32(col_f[...], columns[p]) * kernel_t[ch, p].astype(F32)).astype(BF16)
            back = dot32(col_t[...], spectral)
            columns[p] = (back * column(twiddle_c[...], p)).astype(BF16)

        @pl.loop(0, 16)
        def _(i):
            block = (seq // 2 + 1 + i) % 16
            rows = pl.ds(pl.multiple_of(block * 16, 16), 16)
            turned = dot32(swap[...], columns[:, rows].reshape(256, 256)).astype(BF16)
            send_c[ch, rows] = turned.reshape(16, 16, 256)
            for to_core in range(2):
                to_seq = block * 2 + to_core
                src = send_c.at[ch, pl.ds(pl.multiple_of(to_seq * 8, 8), 8)]
                dst = recv_c.at[ch, :, pl.ds(pl.multiple_of(seq * 16, 16), 16)]

                @pl.when(to_seq == seq)
                def _(src=src, dst=dst):
                    pltpu.make_async_copy(src, dst, c_own.at[ch]).start()

                @pl.when(to_seq != seq)
                def _(src=src, dst=dst, to_seq=to_seq):
                    pltpu.make_async_remote_copy(
                        src_ref=src,
                        dst_ref=dst,
                        send_sem=c_send,
                        recv_sem=c_recv.at[ch],
                        device_id=(to_seq, mp),
                        device_id_type=MESH,
                    ).start()

    wait_bytes(recv_a.at[pl.ds(0, 7)], a_send)

    def out_copy(ch, a):
        lanes = pl.ds(256 * ch, 256)
        return pltpu.make_async_copy(
            send_a.at[a, :, lanes],
            out_hbm.at[pl.ds(pl.multiple_of(a * 512, 512), 512), lanes],
            out_sem.at[ch, a],
        )


    for ch in range(2):
        wait_bytes(recv_c.at[ch, :, pl.ds(0, 496)], c_recv.at[ch])
        wait_bytes(recv_c.at[ch, :, pl.ds(0, 16)], c_own.at[ch])

        @pl.loop(0, 8)
        def _(a):
            cut = slice(256 * ch, 256 * ch + 256)
            total = dot32(row_t[...], recv_c[ch, a])
            send_a[a, :, cut] = (xw[a, 16:, cut].astype(F32) + total).astype(BF16)
            out_copy(ch, a).start()

    for ch in range(2):

        @pl.loop(0, 8)
        def _(a):
            out_copy(ch, a).wait()

    halo.wait_send()
    to_pair.wait_send()
    wait_bytes(left_all.at[pl.ds(0, 7), pl.ds(0, 2)], left_send)
    for ch in range(2):

        @pl.when(z_lo == 1)
        def _():
            wait_bytes(recv_b.at[ch, pl.ds(0, 254)], b_send.at[ch])

        @pl.when(z_lo == 0)
        def _():
            wait_bytes(recv_b.at[ch], b_send.at[ch])

    wait_bytes(recv_c.at[0, :, pl.ds(0, 496)], c_send)
    wait_bytes(recv_c.at[1, :, pl.ds(0, 496)], c_send)


def shards(
    activations,
    conv_weight,
    chan_right,
    chan_left,
    row_factor,
    col_factor,
    twiddle_one,
    twiddle_two,
    spectrum,
):
    hbm = pl.BlockSpec(memory_space=pltpu.HBM)
    dma = pltpu.SemaphoreType.DMA
    scratch = [
        ((8, 528, 512), BF16),
        ((3, 512), F32),
        ((8, 512), F32),
        ((16, 256), F32),
        ((512, 64), BF16),
        ((8, 64, 64), BF16),
        ((4, 64, 128), BF16),
        ((8, 4, 64, 128), BF16),
        ((512, 512), BF16),
        ((512, 512), BF16),
        ((256, 256), BF16),
        ((256, 256), BF16),
        ((256, 256), BF16),
        ((512, 512), BF16),
        ((512, 512), BF16),
        ((4, 8, 128, 1024), BF16),
        ((512, 8), F32),
        ((512, 8), F32),
        ((256, 16), F32),
        ((8, 512, 512), BF16),
        ((8, 2, 256, 512), BF16),
        ((512, 1024), BF16),
        ((2, 8, 2, 256, 256), BF16),
        ((2, 256, 16, 256), BF16),
        ((16, 256, 256), BF16),
        ((2, 16, 256, 256), BF16),
        ((2, 256, 16, 256), BF16),
        ((2, 8, 512, 256), BF16),
    ]
    sems = [(9,), (16,), (8,), (8,), (), (), (), (), (), (), (), (4,), (), (2,), (2,), (2,), (), (2,), (2,), (2, 8)]
    return pl.pallas_call(
        kernel,
        name="monarch",
        out_shape=jax.ShapeDtypeStruct(activations.shape, activations.dtype),
        in_specs=[hbm] * 9,
        out_specs=hbm,
        scratch_shapes=[pltpu.VMEM(*one) for one in scratch]
        + [pltpu.SemaphoreType.REGULAR]
        + [dma(shape) if shape else dma for shape in sems],
        compiler_params=pltpu.CompilerParams(
            collective_id=0, has_side_effects=True, vmem_limit_bytes=60 << 20
        ),
    )(
        activations,
        conv_weight,
        chan_right.reshape(512, 64),
        chan_left,
        row_factor,
        col_factor,
        twiddle_one,
        twiddle_two.T,
        spectrum,
    )


def solution(mesh):
    in_specs = (
        P("seq", "mp"),
        P(None, "mp"),
        P("mp", None, None),
        P("mp", None, None),
        P(),
        P(),
        P("seq", None),
        P(None, "seq"),
        P(None, "seq", "mp"),
    )
    out_specs = P("seq", "mp")
    return jax.shard_map(shards, mesh=mesh, in_specs=in_specs, out_specs=out_specs, check_vma=False)
```
